32 devices in a mesh: rcv: 8 (over y, x, core), win: 4 (over z).
Axes of the slice: x: 2, y: 2, z: 4, core: 2. Of those that a mesh axis runs over, the one named last changes fastest.
Arguments:
- traces: bfloat16 [4096, 4, 6144], P('rcv', 'win'), may hold values from -6 to 6
- sources: int32 [8, 4], replicated, may hold values from 0 to 4095
- offsets: int32 [4], P('win'), may hold values from 0 to 44
Outputs:
- stacks: float32 [32, 101, 4096], P('win', None, 'rcv')
The draws below stay inside these ranges and needn't reach their ends.
All inputs are finite; a program needn't handle non-finite values.
Results may differ from the reference program's by a relative error of at most 0.0003.
Values may be sent and summed in bfloat16 or wider, within the bound.
A program may use at most 192 MiB of HBM per device.

```python
import math
import jax
import jax.numpy as jnp
from jax import lax

SAMPLES = 6000
HALF = 50
PAD = 44
STEPS = 8
SRC = 4
LAGS = 101
SPAN = 6144
CHANNELS = 4096
WINDOWS = 4


def touch_ends(array, stream_key, least, high):
    longest = array.shape.index(max(array.shape))
    spots = []
    for shift in (0, 1):
        where = [jax.random.randint(jax.random.fold_in(stream_key, axis), (), 0, length) for axis, length in enumerate(array.shape)]
        where[longest] = (where[longest] + shift) % array.shape[longest]
        spots.append(tuple(where))
    return array.at[spots[0]].set(least).at[spots[1]].set(high)


def shard_levels(stream_key, extent, cuts, least, largest):
    level = 1.0
    for position, shards_of in cuts:
        steps = jax.random.uniform(jax.random.fold_in(jax.random.fold_in(stream_key, 6), position), (shards_of,), jnp.float32, least / len(cuts), largest / len(cuts))
        level = level * jnp.repeat(jnp.exp(steps), extent[position] // shards_of).reshape((-1,) + (1,) * (len(extent) - 1 - position))
    return level


def scatter_about(rng, shape, scale, limit, split=(), kind=jnp.bfloat16):
    values = jax.random.normal(rng, shape, jnp.float32) * scale
    if len(split) > 0:
        values = shard_levels(rng, shape, split, -0.22, 0.18) * values
    return jnp.clip(values, min=-limit, max=limit).astype(kind)


def setup_inputs(seed: int = 0) -> dict:
    key_of = jax.random.split(jax.random.key(seed), 4)
    traces = scatter_about(key_of[0], (CHANNELS, WINDOWS, SPAN), 1.0, 6.0, ((0, 8), (1, 4)))
    sources = touch_ends(jax.random.randint(key_of[1], (STEPS, SRC), 0, CHANNELS), jax.random.fold_in(key_of[1], 1), 0, CHANNELS - 1).astype(jnp.int32)
    offsets = touch_ends(jax.random.randint(key_of[2], (WINDOWS,), 0, PAD + 1), jax.random.fold_in(key_of[2], 1), 0, PAD).astype(jnp.int32)
    return {"traces": traces, "sources": sources, "offsets": offsets}


def lagged(signal):
    leading = signal.shape[:-1]
    padded = jnp.concatenate([signal, jnp.zeros(leading + (2 * HALF + 1,), signal.dtype)], axis=-1)
    span_len = padded.shape[-1]
    tiled = jnp.tile(padded, (1,) * len(leading) + (LAGS,))
    return tiled[..., :LAGS * (span_len - 1)].reshape(leading + (LAGS, span_len - 1))

def reference(traces, sources, offsets):
    source_all = traces[sources.reshape(-1).astype(jnp.int32)]

    def one_window(summed, window):
        start_at = offsets[window].astype(jnp.int32)
        source_win = lax.dynamic_index_in_dim(source_all, window, 1, keepdims=False)
        trace_win = lax.dynamic_index_in_dim(traces, window, 1, keepdims=False)
        source_cut = lax.dynamic_slice_in_dim(source_win, start_at + HALF, SAMPLES, 1)
        receiver = lax.dynamic_slice_in_dim(trace_win, start_at, SAMPLES + 2 * HALF, 1)
        term = jnp.einsum('kjt,ct->kjc', lagged(source_cut).astype(jnp.float32), receiver.astype(jnp.float32))
        return (summed + term, None)
    initial = jnp.zeros((STEPS * SRC, LAGS, CHANNELS), jnp.float32)
    summed, _ = lax.scan(one_window, initial, jnp.arange(WINDOWS, dtype=jnp.int32))
    return summed * (1.0 / math.sqrt(SAMPLES * WINDOWS))
```

```python
import functools
import math

import jax
import jax.numpy as jnp
from jax import lax
from jax.experimental import pallas as pl
from jax.experimental.pallas import tpu as pltpu
from jax.sharding import PartitionSpec as P

SAMPLES = 6000
HALF = 50
LAGS = 101
ROWS = 104
LEAD = 128
TOP = 32766.0


def code(total):
    row = lax.broadcasted_iota(jnp.int32, total.shape, 0)
    largest = jnp.max(jnp.where(row < LAGS, jnp.abs(total), 0.0), axis=0, keepdims=True)
    level = jnp.ceil(jnp.log2(jnp.maximum(largest, 1e-30)) * 16.0) + 1.0
    scaled = jnp.round(total * (jnp.exp2(level * (-1.0 / 16.0)) * TOP))
    return jnp.where(row == LAGS, level, jnp.where(row < LAGS, scaled, 0.0)).astype(jnp.int32)


def decode(coded):
    values = coded.astype(jnp.float32)
    return values * (jnp.exp2(values[LAGS : LAGS + 1] * (1.0 / 16.0)) * (1.0 / TOP))


def kernel(windows, norm_scale, depth, source_ref, trace_ref, out_ref, total, sent, landed, send_sem, recv_sem):
    place = lax.axis_index("win")
    per_group = source_ref.shape[0] // (2 * windows)
    span_len = trace_ref.shape[0]

    barrier = pltpu.get_barrier_semaphore()

    @pl.when(place > 0)
    def _():
        pl.semaphore_signal(barrier, inc=1, device_id={"win": place - 1}, device_id_type=pl.DeviceIdType.MESH)

    @pl.when(place < windows - 1)
    def _():
        pl.semaphore_signal(barrier, inc=1, device_id={"win": place + 1}, device_id_type=pl.DeviceIdType.MESH)

    pl.semaphore_wait(barrier, jnp.where(place > 0, 1, 0) + jnp.where(place < windows - 1, 1, 0))

    def correlate(pair):
        total[...] = jnp.zeros_like(total)

        @pl.loop(0, span_len // depth)
        def _(piece):
            begin = pl.multiple_of(piece * depth, depth)
            lags = []
            for member in range(2):
                record = source_ref[pl.ds(2 * pair + member, 1), pl.ds(begin, LEAD + depth)]
                spread = jnp.broadcast_to(record, (ROWS, LEAD + depth))
                lags.append(pltpu.roll(spread, 0, 1, stride=1, stride_axis=0)[:, LEAD:])
            shifted = jnp.concatenate(lags, axis=0).astype(jnp.bfloat16)
            total[...] += jnp.dot(shifted, trace_ref[pl.ds(begin, depth), :], preferred_element_type=jnp.float32)

        total[...] *= norm_scale

    def landing(way, pair):
        return pltpu.make_async_remote_copy(
            src_ref=sent.at[pair],
            dst_ref=landed.at[way, pair],
            send_sem=send_sem.at[pair],
            recv_sem=recv_sem.at[way, pair],
            device_id={"win": place + 1 - 2 * way},
            device_id_type=pl.DeviceIdType.MESH,
        )

    def add_landed(way, pair):
        landing(way, pair).wait_recv()
        for member in range(2):
            rows = slice(member * ROWS, (member + 1) * ROWS)
            total[rows] += decode(landed[way, pair].astype(jnp.int32)[rows])

    @pl.loop(0, 2 * (windows - 1) * per_group)
    def _(slot):
        stage = slot // (2 * per_group)
        inner = lax.rem(slot // 2, per_group)
        way = lax.rem(slot, 2)
        group = jnp.where(way == 0, windows - 1 - stage, stage)
        active = jnp.where(way == 0, group > place, group < place)

        @pl.when(active)
        def _():
            pair = group * per_group + inner
            correlate(pair)

            @pl.when(jnp.where(way == 0, place > 0, place < windows - 1))
            def _():
                add_landed(way, pair)

            coded = [code(total[member * ROWS : (member + 1) * ROWS]) for member in range(2)]
            sent[pair] = jnp.concatenate(coded, axis=0).astype(jnp.int16)
            landing(way, pair).start()

    @pl.loop(0, per_group)
    def _(inner):
        pair = place * per_group + inner
        correlate(pair)

        @pl.when(place > 0)
        def _():
            add_landed(0, pair)

        @pl.when(place < windows - 1)
        def _():
            add_landed(1, pair)

        for member in range(2):
            out_ref[2 * inner + member] = total[member * ROWS : member * ROWS + LAGS]

    @pl.loop(0, windows * per_group)
    def _(pair):
        @pl.when(pair // per_group != place)
        def _():
            landing(0, pair).wait_send()


def shards(traces, sources, offsets):
    ch_dev = traces.shape[0]
    span_len = traces.shape[2]
    source_count = sources.size
    windows = lax.axis_size("win")
    first_row = lax.axis_index("rcv") * ch_dev
    norm_scale = 1.0 / math.sqrt(SAMPLES * windows * traces.shape[1])
    local = traces[:, 0, :]
    wanted = sources.reshape(-1) - first_row
    select = (wanted[:, None] == jnp.arange(ch_dev, dtype=jnp.int32)[None, :]).astype(traces.dtype)
    picked = jnp.dot(select, local, preferred_element_type=jnp.float32).astype(traces.dtype)
    records = lax.psum(picked, "rcv")
    positions = jnp.arange(span_len, dtype=jnp.int32)
    start_at = offsets[0] + HALF
    inside = (positions >= start_at) & (positions < start_at + SAMPLES)
    masked = jnp.where(inside[None, :], records.astype(jnp.float32), 0.0)
    padded = jnp.pad(masked, ((0, 0), (LEAD - HALF, HALF)))
    pairs = source_count // 2
    group = source_count // windows
    return pl.pallas_call(
        functools.partial(kernel, windows, norm_scale, 512),
        out_shape=jax.ShapeDtypeStruct((group, LAGS, ch_dev), jnp.float32),
        in_specs=[pl.BlockSpec(memory_space=pltpu.VMEM)] * 2,
        out_specs=pl.BlockSpec(memory_space=pltpu.VMEM),
        scratch_shapes=[
            pltpu.VMEM((2 * ROWS, ch_dev), jnp.float32),
            pltpu.VMEM((pairs, 2 * ROWS, ch_dev), jnp.int16),
            pltpu.VMEM((2, pairs, 2 * ROWS, ch_dev), jnp.int16),
            pltpu.SemaphoreType.DMA((pairs,)),
            pltpu.SemaphoreType.DMA((2, pairs)),
        ],
        compiler_params=pltpu.CompilerParams(
            collective_id=0, has_side_effects=True, vmem_limit_bytes=56 * 1024 * 1024
        ),
        cost_estimate=pl.CostEstimate(
            flops=2 * source_count * ROWS * ch_dev * span_len,
            bytes_accessed=2 * ch_dev * span_len,
            transcendentals=0,
        ),
    )(padded, local.T)


def solution(mesh):
    in_specs = (P("rcv", "win", None), P(), P("win"))
    out_specs = P("win", None, "rcv")
    return jax.shard_map(shards, mesh=mesh, in_specs=in_specs, out_specs=out_specs, check_vma=False)
```

```python
import functools
import math

import jax
import jax.numpy as jnp
from jax import lax
from jax.experimental import pallas as pl
from jax.experimental.pallas import tpu as pltpu
from jax.sharding import PartitionSpec as P

SAMPLES = 6000
HALF = 50
LAGS = 101
ROWS = 104
LEAD = 128
FOLD = 16
TOP = 32766.0


def code(total):
    row = lax.broadcasted_iota(jnp.int32, total.shape, 0)
    largest = jnp.max(jnp.where(row < LAGS, jnp.abs(total), 0.0), axis=0, keepdims=True)
    level = jnp.ceil(jnp.log2(jnp.maximum(largest, 1e-30)) * 16.0) + 1.0
    scaled = jnp.round(total * (jnp.exp2(level * (-1.0 / 16.0)) * TOP))
    return jnp.where(row == LAGS, level, jnp.where(row < LAGS, scaled, 0.0)).astype(jnp.int32)


def decode(coded):
    values = coded.astype(jnp.float32)
    return values * (jnp.exp2(values[LAGS : LAGS + 1] * (1.0 / 16.0)) * (1.0 / TOP))


def kernel(parts, windows, norm_scale, members, depth, source_ids, offset_ref, trace_hbm, out_ref,
           trace, packed, met, found, rows, padded, total, sent, landed,
           load_sem, meet_send, meet_recv, find_send, find_recv, send_sem, recv_sem):
    place = lax.axis_index("win")
    own = lax.axis_index("rcv")
    ch_dev, span_len = trace.shape
    source_count = rows.shape[0]
    per_part = source_count // parts
    slabs = FOLD // per_part
    width = span_len // slabs
    quads = source_count // (members * windows)
    last = windows - 1

    def load(slab):
        columns = pl.ds(slab * width, width)
        return pltpu.make_async_copy(trace_hbm.at[:, columns], trace.at[:, columns], load_sem.at[slab])

    for slab in range(slabs):
        load(slab).start()

    def greet(coordinates):
        pl.semaphore_signal(barrier, inc=1, device_id=coordinates, device_id_type=pl.DeviceIdType.MESH)

    barrier = pltpu.get_barrier_semaphore()
    for hop in range(1, parts):
        greet({"rcv": lax.rem(own + hop, parts)})

    @pl.when(place > 0)
    def _():
        greet({"win": place - 1})

    @pl.when(place < last)
    def _():
        greet({"win": place + 1})

    row = lax.broadcasted_iota(jnp.int32, (parts * FOLD, ch_dev), 0)
    channel = lax.broadcasted_iota(jnp.int32, (parts * FOLD, ch_dev), 1) + own * ch_dev
    source_of = (row // FOLD) * per_part + lax.rem(row, per_part)
    slab_of = lax.rem(row, FOLD) // per_part
    wanted = jnp.zeros(row.shape, jnp.int32)
    group_size = source_count // source_ids.shape[0]
    for source in range(source_count):
        wanted = jnp.where(source_of == source, source_ids[source // group_size, source % group_size], wanted)
    picked = jnp.zeros((parts * FOLD, width), jnp.float32)
    for slab in range(slabs):
        load(slab).wait()
        select = jnp.where((wanted == channel) & (slab_of == slab), 1.0, 0.0).astype(trace.dtype)
        picked += jnp.dot(select, trace[:, slab * width : (slab + 1) * width], preferred_element_type=jnp.float32)
    packed[...] = picked.astype(packed.dtype).reshape(packed.shape)

    pl.semaphore_wait(barrier, parts - 1 + jnp.where(place > 0, 1, 0) + jnp.where(place < last, 1, 0))

    def meet(hop):
        peer = lax.rem(own + hop, parts)
        return pltpu.make_async_remote_copy(
            src_ref=packed.at[peer], dst_ref=met.at[hop - 1], send_sem=meet_send.at[hop - 1],
            recv_sem=meet_recv.at[hop - 1], device_id={"rcv": peer}, device_id_type=pl.DeviceIdType.MESH)

    def find(hop):
        peer = lax.rem(own + hop, parts)
        return pltpu.make_async_remote_copy(
            src_ref=found.at[own], dst_ref=found.at[own], send_sem=find_send.at[hop - 1],
            recv_sem=find_recv.at[hop - 1], device_id={"rcv": peer}, device_id_type=pl.DeviceIdType.MESH)

    for hop in range(1, parts):
        meet(hop).start()
    record = packed[own].astype(jnp.float32)
    for hop in range(1, parts):
        meet(hop).wait_recv()
        record += met[hop - 1].astype(jnp.float32)
    found[own] = record.astype(found.dtype)
    for hop in range(1, parts):
        find(hop).start()
    for hop in range(1, parts):
        find(hop).wait_recv()
    for part in range(parts):
        block = found[part].astype(jnp.float32)
        for slab in range(slabs):
            rows[part * per_part : (part + 1) * per_part, slab * width : (slab + 1) * width] = block[
                slab * per_part : (slab + 1) * per_part
            ]
    position = lax.broadcasted_iota(jnp.int32, rows.shape, 1)
    start_at = offset_ref[0] + HALF
    masked = jnp.where((position >= start_at) & (position < start_at + SAMPLES), rows[...], 0.0)
    padded[...] = pltpu.roll(
        jnp.concatenate([masked, jnp.zeros((source_count, LEAD), jnp.float32)], axis=1), LEAD - HALF, 1
    )

    def correlate(quad):
        total[...] = jnp.zeros_like(total)

        @pl.loop(0, span_len // depth)
        def _(piece):
            begin = pl.multiple_of(piece * depth, depth)
            lags = []
            for member in range(members):
                line = padded[pl.ds(members * quad + member, 1), pl.ds(begin, LEAD + depth)]
                spread = jnp.broadcast_to(line, (ROWS, LEAD + depth))
                lags.append(pltpu.roll(spread, 0, 1, stride=1, stride_axis=0)[:, LEAD:])
            shifted = jnp.concatenate(lags, axis=0).astype(jnp.bfloat16)
            total[...] += lax.dot_general(
                shifted, trace[:, pl.ds(begin, depth)], (((1,), (1,)), ((), ())), preferred_element_type=jnp.float32
            )

        total[...] *= norm_scale

    pairs_in = members // 2

    def landing(way, pair):
        return pltpu.make_async_remote_copy(
            src_ref=sent.at[pair],
            dst_ref=landed.at[way, pair],
            send_sem=send_sem.at[pair],
            recv_sem=recv_sem.at[way, pair],
            device_id={"win": place + 1 - 2 * way},
            device_id_type=pl.DeviceIdType.MESH,
        )

    def add_landed(way, pair, base):
        landing(way, pair).wait_recv()
        coded = landed[way, pair].astype(jnp.int32)
        for member in range(2):
            total[base + member * ROWS : base + (member + 1) * ROWS] += decode(coded[member * ROWS : (member + 1) * ROWS])

    @pl.loop(0, 2 * last * quads)
    def _(slot):
        stage = slot // (2 * quads)
        inner = lax.rem(slot // 2, quads)
        way = lax.rem(slot, 2)
        group = jnp.where(way == 0, last - stage, stage)

        @pl.when(jnp.where(way == 0, group > place, group < place))
        def _():
            quad = group * quads + inner
            correlate(quad)
            for half in range(pairs_in):
                pair = quad * pairs_in + half
                base = half * 2 * ROWS

                @pl.when(jnp.where(way == 0, place > 0, place < last))
                def _():
                    add_landed(way, pair, base)

                coded = [code(total[base + member * ROWS : base + (member + 1) * ROWS]) for member in range(2)]
                sent[pair] = jnp.concatenate(coded, axis=0).astype(jnp.int16)
                landing(way, pair).start()

    @pl.loop(0, quads)
    def _(inner):
        quad = place * quads + inner
        correlate(quad)
        for half in range(pairs_in):
            pair = quad * pairs_in + half
            base = half * 2 * ROWS

            @pl.when(place > 0)
            def _():
                add_landed(0, pair, base)

            @pl.when(place < last)
            def _():
                add_landed(1, pair, base)

        for member in range(members):
            out_ref[members * inner + member] = total[member * ROWS : member * ROWS + LAGS]

    for hop in range(1, parts):
        meet(hop).wait_send()
        find(hop).wait_send()

    @pl.loop(0, source_count // 2)
    def _(pair):
        @pl.when(pair // (quads * pairs_in) != place)
        def _():
            landing(0, pair).wait_send()


def shards(traces, sources, offsets):
    ch_dev, win_dev, span_len = traces.shape
    source_count = sources.size
    windows = lax.axis_size("win")
    parts = lax.axis_size("rcv")
    norm_scale = 1.0 / math.sqrt(SAMPLES * windows * win_dev)
    members = 4
    slabs = FOLD * parts // source_count
    width = span_len // slabs
    pairs = source_count // 2
    group = source_count // windows
    return pl.pallas_call(
        functools.partial(kernel, parts, windows, norm_scale, members, 2048),
        out_shape=jax.ShapeDtypeStruct((group, LAGS, ch_dev), jnp.float32),
        in_specs=[
            pl.BlockSpec(memory_space=pltpu.SMEM),
            pl.BlockSpec(memory_space=pltpu.SMEM),
            pl.BlockSpec(memory_space=pl.ANY),
        ],
        out_specs=pl.BlockSpec(memory_space=pltpu.VMEM),
        scratch_shapes=[
            pltpu.VMEM((ch_dev, span_len), traces.dtype),
            pltpu.VMEM((parts, FOLD, width), traces.dtype),
            pltpu.VMEM((parts - 1, FOLD, width), traces.dtype),
            pltpu.VMEM((parts, FOLD, width), traces.dtype),
            pltpu.VMEM((source_count, span_len), jnp.float32),
            pltpu.VMEM((source_count, span_len + LEAD), jnp.float32),
            pltpu.VMEM((members * ROWS, ch_dev), jnp.float32),
            pltpu.VMEM((pairs, 2 * ROWS, ch_dev), jnp.int16),
            pltpu.VMEM((2, pairs, 2 * ROWS, ch_dev), jnp.int16),
            pltpu.SemaphoreType.DMA((slabs,)),
            pltpu.SemaphoreType.DMA((parts - 1,)),
            pltpu.SemaphoreType.DMA((parts - 1,)),
            pltpu.SemaphoreType.DMA((parts - 1,)),
            pltpu.SemaphoreType.DMA((parts - 1,)),
            pltpu.SemaphoreType.DMA((pairs,)),
            pltpu.SemaphoreType.DMA((2, pairs)),
        ],
        compiler_params=pltpu.CompilerParams(
            collective_id=0, has_side_effects=True, vmem_limit_bytes=56 * 1024 * 1024
        ),
        cost_estimate=pl.CostEstimate(
            flops=2 * source_count * ROWS * ch_dev * span_len,
            bytes_accessed=2 * ch_dev * span_len,
            transcendentals=0,
        ),
    )(sources, offsets, traces.reshape(ch_dev, span_len))


def solution(mesh):
    in_specs = (P("rcv", "win", None), P(), P("win"))
    out_specs = P("win", None, "rcv")
    return jax.shard_map(shards, mesh=mesh, in_specs=in_specs, out_specs=out_specs, check_vma=False)
```

```python
import functools
import math

import jax
import jax.numpy as jnp
from jax import lax
from jax.experimental import pallas as pl
from jax.experimental.pallas import tpu as pltpu
from jax.sharding import PartitionSpec as P

SAMPLES = 6000
HALF = 50
LAGS = 101
ROWS = 104
LEAD = 128
FOLD = 16
AHEAD = 2
TOP = 32766.0


def code(total):
    row = lax.broadcasted_iota(jnp.int32, total.shape, 0)
    largest = jnp.max(jnp.where(row < LAGS, jnp.abs(total), 0.0), axis=0, keepdims=True)
    level = jnp.ceil(jnp.log2(jnp.maximum(largest, 1e-30)) * 16.0) + 1.0
    scaled = jnp.round(total * (jnp.exp2(level * (-1.0 / 16.0)) * TOP))
    return jnp.where(row == LAGS, level, jnp.where(row < LAGS, scaled, 0.0)).astype(jnp.int32)


def decode(coded):
    values = coded.astype(jnp.float32)
    return values * (jnp.exp2(values[LAGS : LAGS + 1] * (1.0 / 16.0)) * (1.0 / TOP))


def kernel(parts, windows, norm_scale, members, depth, source_ids, offset_ref, trace_hbm, out_ref,
           trace, packed, met, found, rows, padded, total, sent, landed,
           load_sem, meet_send, meet_recv, find_send, find_recv, send_sem, recv_sem):
    place = lax.axis_index("win")
    own = lax.axis_index("rcv")
    ch_dev, span_len = trace.shape
    source_count = rows.shape[0]
    per_part = source_count // parts
    slabs = FOLD // per_part
    width = span_len // slabs
    quads = source_count // (members * windows)
    last = windows - 1

    def load(slab):
        columns = pl.ds(slab * width, width)
        return pltpu.make_async_copy(trace_hbm.at[:, columns], trace.at[:, columns], load_sem.at[slab])

    for slab in range(slabs):
        load(slab).start()

    def greet(coordinates):
        pl.semaphore_signal(barrier, inc=1, device_id=coordinates, device_id_type=pl.DeviceIdType.MESH)

    barrier = pltpu.get_barrier_semaphore()
    for hop in range(1, parts):
        greet({"rcv": lax.rem(own + hop, parts)})

    @pl.when(place > 0)
    def _():
        greet({"win": place - 1})

    @pl.when(place < last)
    def _():
        greet({"win": place + 1})

    row = lax.broadcasted_iota(jnp.int32, (parts * FOLD, ch_dev), 0)
    channel = lax.broadcasted_iota(jnp.int32, (parts * FOLD, ch_dev), 1) + own * ch_dev
    source_of = (row // FOLD) * per_part + lax.rem(row, per_part)
    slab_of = lax.rem(row, FOLD) // per_part
    wanted = jnp.zeros(row.shape, jnp.int32)
    group_size = source_ids.shape[0]
    for source in range(source_count):
        wanted = jnp.where(source_of == source, source_ids[source % group_size, source // group_size], wanted)
    picked = jnp.zeros((parts * FOLD, width), jnp.float32)
    for slab in range(slabs):
        load(slab).wait()
        select = jnp.where((wanted == channel) & (slab_of == slab), 1.0, 0.0).astype(trace.dtype)
        picked += jnp.dot(select, trace[:, slab * width : (slab + 1) * width], preferred_element_type=jnp.float32)
    packed[...] = picked.astype(packed.dtype).reshape(packed.shape)

    pl.semaphore_wait(barrier, parts - 1 + jnp.where(place > 0, 1, 0) + jnp.where(place < last, 1, 0))

    def meet(hop):
        peer = lax.rem(own + hop, parts)
        return pltpu.make_async_remote_copy(
            src_ref=packed.at[peer], dst_ref=met.at[hop - 1], send_sem=meet_send.at[hop - 1],
            recv_sem=meet_recv.at[hop - 1], device_id={"rcv": peer}, device_id_type=pl.DeviceIdType.MESH)

    def find(hop):
        peer = lax.rem(own + hop, parts)
        return pltpu.make_async_remote_copy(
            src_ref=found.at[own], dst_ref=found.at[own], send_sem=find_send.at[hop - 1],
            recv_sem=find_recv.at[hop - 1], device_id={"rcv": peer}, device_id_type=pl.DeviceIdType.MESH)

    for hop in range(1, parts):
        meet(hop).start()
    record = packed[own].astype(jnp.float32)
    for hop in range(1, parts):
        meet(hop).wait_recv()
        record += met[hop - 1].astype(jnp.float32)
    found[own] = record.astype(found.dtype)
    for hop in range(1, parts):
        find(hop).start()
    for hop in range(1, parts):
        find(hop).wait_recv()
    for part in range(parts):
        block = found[part].astype(jnp.float32)
        for slab in range(slabs):
            rows[part * per_part : (part + 1) * per_part, slab * width : (slab + 1) * width] = block[
                slab * per_part : (slab + 1) * per_part
            ]
    position = lax.broadcasted_iota(jnp.int32, rows.shape, 1)
    start_at = offset_ref[0] + HALF
    masked = jnp.where((position >= start_at) & (position < start_at + SAMPLES), rows[...], 0.0)
    padded[...] = pltpu.roll(
        jnp.concatenate([masked, jnp.zeros((source_count, LEAD), jnp.float32)], axis=1), LEAD - HALF, 1
    )

    def correlate(quad, slot):
        total[slot] = jnp.zeros(total.shape[1:], total.dtype)

        @pl.loop(0, span_len // depth)
        def _(piece):
            begin = pl.multiple_of(piece * depth, depth)
            lags = []
            for member in range(members):
                line = padded[pl.ds(members * quad + member, 1), pl.ds(begin, LEAD + depth)]
                spread = jnp.broadcast_to(line, (ROWS, LEAD + depth))
                lags.append(pltpu.roll(spread, 0, 1, stride=1, stride_axis=0)[:, LEAD:])
            shifted = jnp.concatenate(lags, axis=0).astype(jnp.bfloat16)
            total[slot] += lax.dot_general(
                shifted, trace[:, pl.ds(begin, depth)], (((1,), (1,)), ((), ())), preferred_element_type=jnp.float32
            )

        total[slot] *= norm_scale

    pairs_in = members // 2
    per_group = quads * pairs_in

    def landing(way, pair):
        return pltpu.make_async_remote_copy(
            src_ref=sent.at[pair],
            dst_ref=landed.at[way, pair],
            send_sem=send_sem.at[pair],
            recv_sem=recv_sem.at[way, pair],
            device_id={"win": place + 1 - 2 * way},
            device_id_type=pl.DeviceIdType.MESH,
        )

    def add_landed(way, pair, slot, base):
        landing(way, pair).wait_recv()
        coded = landed[way, pair].astype(jnp.int32)
        for member in range(2):
            part_rows = slice(base + member * ROWS, base + (member + 1) * ROWS)
            total[slot, part_rows] += decode(coded[member * ROWS : (member + 1) * ROWS])

    def pair_at(way, turn):
        group = jnp.where(way == 0, last - turn // per_group, turn // per_group)
        return group * per_group + lax.rem(turn, per_group)

    between = (place > 0) & (place < last)
    first_way = jnp.where(2 * place < windows, 0, 1)

    @pl.when(between)
    def _():
        @pl.loop(0, quads)
        def _(inner):
            correlate(place * quads + inner, inner)

    @pl.loop(0, 2 * last * quads)
    def _(slot):
        stage = slot // (2 * quads)
        inner = lax.rem(slot // 2, quads)
        way = lax.rem(slot + first_way, 2)
        group = jnp.where(way == 0, last - stage, stage)

        @pl.when(jnp.where(way == 0, group > place, group < place))
        def _():
            quad = group * quads + inner
            correlate(quad, quads)
            for half in range(pairs_in):
                pair = quad * pairs_in + half
                turn = (stage * quads + inner) * pairs_in + half
                base = half * 2 * ROWS

                @pl.when(jnp.where(way == 0, place > 0, place < last))
                def _():
                    add_landed(way, pair, quads, base)

                coded = [code(total[quads, base + member * ROWS : base + (member + 1) * ROWS]) for member in range(2)]
                sent[pair] = jnp.concatenate(coded, axis=0).astype(jnp.int16)

                @pl.when(turn >= AHEAD)
                def _():
                    landing(way, pair_at(way, turn - AHEAD)).wait_send()

                landing(way, pair).start()

    @pl.when(jnp.logical_not(between))
    def _():
        @pl.loop(0, quads)
        def _(inner):
            correlate(place * quads + inner, inner)

    @pl.loop(0, quads)
    def _(inner):
        for half in range(pairs_in):
            pair = (place * quads + inner) * pairs_in + half
            base = half * 2 * ROWS

            @pl.when(place > 0)
            def _():
                add_landed(0, pair, inner, base)

            @pl.when(place < last)
            def _():
                add_landed(1, pair, inner, base)

        for member in range(members):
            out_ref[members * inner + member] = total[inner, member * ROWS : member * ROWS + LAGS]

    for hop in range(1, parts):
        meet(hop).wait_send()
        find(hop).wait_send()

    for way in range(2):
        turns = (place if way else last - place) * per_group

        @pl.loop(0, last * per_group)
        def _(turn):
            @pl.when((turn < turns) & (turn >= turns - AHEAD))
            def _():
                landing(way, pair_at(way, turn)).wait_send()


def shards(traces, sources, offsets):
    ch_dev, win_dev, span_len = traces.shape
    source_count = sources.size
    windows = lax.axis_size("win")
    parts = lax.axis_size("rcv")
    norm_scale = 1.0 / math.sqrt(SAMPLES * windows * win_dev)
    members = 4
    slabs = FOLD * parts // source_count
    width = span_len // slabs
    pairs = source_count // 2
    group = source_count // windows
    return pl.pallas_call(
        functools.partial(kernel, parts, windows, norm_scale, members, 2048),
        out_shape=jax.ShapeDtypeStruct((group, LAGS, ch_dev), jnp.float32),
        in_specs=[
            pl.BlockSpec(memory_space=pltpu.SMEM),
            pl.BlockSpec(memory_space=pltpu.SMEM),
            pl.BlockSpec(memory_space=pl.ANY),
        ],
        out_specs=pl.BlockSpec(memory_space=pltpu.VMEM),
        scratch_shapes=[
            pltpu.VMEM((ch_dev, span_len), traces.dtype),
            pltpu.VMEM((parts, FOLD, width), traces.dtype),
            pltpu.VMEM((parts - 1, FOLD, width), traces.dtype),
            pltpu.VMEM((parts, FOLD, width), traces.dtype),
            pltpu.VMEM((source_count, span_len), jnp.float32),
            pltpu.VMEM((source_count, span_len + LEAD), jnp.float32),
            pltpu.VMEM((group // members + 1, members * ROWS, ch_dev), jnp.float32),
            pltpu.VMEM((pairs, 2 * ROWS, ch_dev), jnp.int16),
            pltpu.VMEM((2, pairs, 2 * ROWS, ch_dev), jnp.int16),
            pltpu.SemaphoreType.DMA((slabs,)),
            pltpu.SemaphoreType.DMA((parts - 1,)),
            pltpu.SemaphoreType.DMA((parts - 1,)),
            pltpu.SemaphoreType.DMA((parts - 1,)),
            pltpu.SemaphoreType.DMA((parts - 1,)),
            pltpu.SemaphoreType.DMA((pairs,)),
            pltpu.SemaphoreType.DMA((2, pairs)),
        ],
        compiler_params=pltpu.CompilerParams(
            collective_id=0, has_side_effects=True, vmem_limit_bytes=56 * 1024 * 1024
        ),
        cost_estimate=pl.CostEstimate(
            flops=2 * source_count * ROWS * ch_dev * span_len,
            bytes_accessed=2 * ch_dev * span_len,
            transcendentals=0,
        ),
    )(sources.T, offsets, traces.reshape(ch_dev, span_len))


def solution(mesh):
    in_specs = (P("rcv", "win", None), P(), P("win"))
    out_specs = P("win", None, "rcv")
    return jax.shard_map(shards, mesh=mesh, in_specs=in_specs, out_specs=out_specs, check_vma=False)
```

```python
import functools
import math

import jax
import jax.numpy as jnp
from jax import lax
from jax.experimental import pallas as pl
from jax.experimental.pallas import tpu as pltpu
from jax.sharding import PartitionSpec as P

SAMPLES = 6000
HALF = 50
LAGS = 101
ROWS = 104
LEAD = 128
FOLD = 16
AHEAD = 2
TOP = 32766.0


def code(total):
    row = lax.broadcasted_iota(jnp.int32, total.shape, 0)
    largest = jnp.max(jnp.where(row < LAGS, jnp.abs(total), 0.0), axis=0, keepdims=True)
    level = jnp.ceil(jnp.log2(jnp.maximum(largest, 1e-30)) * 16.0) + 1.0
    scaled = jnp.round(total * (jnp.exp2(level * (-1.0 / 16.0)) * TOP))
    return jnp.where(row == LAGS, level, jnp.where(row < LAGS, scaled, 0.0)).astype(jnp.int32)


def decode(coded):
    values = coded.astype(jnp.float32)
    return values * (jnp.exp2(values[LAGS : LAGS + 1] * (1.0 / 16.0)) * (1.0 / TOP))


def kernel(parts, windows, norm_scale, members, depth, source_ids, offset_ref, trace_hbm, out_ref,
           trace, packed, met, found, rows, padded, total, sent, landed,
           load_sem, meet_send, meet_recv, find_send, find_recv, send_sem, recv_sem):
    place = lax.axis_index("win")
    own = lax.axis_index("rcv")
    ch_dev, span_len = trace.shape
    source_count = rows.shape[0]
    per_part = source_count // parts
    slabs = FOLD // per_part
    width = span_len // slabs
    quads = source_count // (members * windows)
    last = windows - 1

    def load(slab):
        columns = pl.ds(slab * width, width)
        return pltpu.make_async_copy(trace_hbm.at[:, columns], trace.at[:, columns], load_sem.at[slab])

    for slab in range(slabs):
        load(slab).start()

    def greet(coordinates):
        pl.semaphore_signal(barrier, inc=1, device_id=coordinates, device_id_type=pl.DeviceIdType.MESH)

    barrier = pltpu.get_barrier_semaphore()
    for hop in range(1, parts):
        greet({"rcv": lax.rem(own + hop, parts)})

    @pl.when(place > 0)
    def _():
        greet({"win": place - 1})

    @pl.when(place < last)
    def _():
        greet({"win": place + 1})

    row = lax.broadcasted_iota(jnp.int32, (parts * FOLD, ch_dev), 0)
    channel = lax.broadcasted_iota(jnp.int32, (parts * FOLD, ch_dev), 1) + own * ch_dev
    source_of = (row // FOLD) * per_part + lax.rem(row, per_part)
    slab_of = lax.rem(row, FOLD) // per_part
    wanted = jnp.zeros(row.shape, jnp.int32)
    group_size = source_ids.shape[0]
    for source in range(source_count):
        wanted = jnp.where(source_of == source, source_ids[source % group_size, source // group_size], wanted)
    picked = jnp.zeros((parts * FOLD, width), jnp.float32)
    for slab in range(slabs):
        load(slab).wait()
        select = jnp.where((wanted == channel) & (slab_of == slab), 1.0, 0.0).astype(trace.dtype)
        picked += jnp.dot(select, trace[:, slab * width : (slab + 1) * width], preferred_element_type=jnp.float32)
    packed[...] = picked.astype(packed.dtype).reshape(packed.shape)

    pl.semaphore_wait(barrier, parts - 1 + jnp.where(place > 0, 1, 0) + jnp.where(place < last, 1, 0))

    def meet(hop):
        peer = lax.rem(own + hop, parts)
        return pltpu.make_async_remote_copy(
            src_ref=packed.at[peer], dst_ref=met.at[hop - 1], send_sem=meet_send.at[hop - 1],
            recv_sem=meet_recv.at[hop - 1], device_id={"rcv": peer}, device_id_type=pl.DeviceIdType.MESH)

    def find(hop):
        peer = lax.rem(own + hop, parts)
        return pltpu.make_async_remote_copy(
            src_ref=found.at[own], dst_ref=found.at[own], send_sem=find_send.at[hop - 1],
            recv_sem=find_recv.at[hop - 1], device_id={"rcv": peer}, device_id_type=pl.DeviceIdType.MESH)

    for hop in range(1, parts):
        meet(hop).start()
    record = packed[own].astype(jnp.float32)
    for hop in range(1, parts):
        meet(hop).wait_recv()
        record += met[hop - 1].astype(jnp.float32)
    found[own] = record.astype(found.dtype)
    for hop in range(1, parts):
        find(hop).start()
    for hop in range(1, parts):
        find(hop).wait_recv()
    for part in range(parts):
        block = found[part].astype(jnp.float32)
        for slab in range(slabs):
            rows[part * per_part : (part + 1) * per_part, slab * width : (slab + 1) * width] = block[
                slab * per_part : (slab + 1) * per_part
            ]
    position = lax.broadcasted_iota(jnp.int32, rows.shape, 1)
    start_at = offset_ref[0] + HALF
    masked = jnp.where((position >= start_at) & (position < start_at + SAMPLES), rows[...], 0.0)
    padded[...] = pltpu.roll(
        jnp.concatenate([masked, jnp.zeros((source_count, LEAD), jnp.float32)], axis=1), LEAD - HALF, 1
    )

    def correlate(quad, slot, least=0, count=members):
        block = slice(least * ROWS, (least + count) * ROWS)
        total[slot, block] = jnp.zeros((count * ROWS, ch_dev), total.dtype)

        @pl.loop(0, span_len // depth)
        def _(piece):
            begin = pl.multiple_of(piece * depth, depth)
            lags = []
            for member in range(least, least + count):
                line = padded[pl.ds(members * quad + member, 1), pl.ds(begin, LEAD + depth)]
                spread = jnp.broadcast_to(line, (ROWS, LEAD + depth))
                lags.append(pltpu.roll(spread, 0, 1, stride=1, stride_axis=0)[:, LEAD:])
            shifted = jnp.concatenate(lags, axis=0).astype(jnp.bfloat16)
            total[slot, block] += lax.dot_general(
                shifted, trace[:, pl.ds(begin, depth)], (((1,), (1,)), ((), ())), preferred_element_type=jnp.float32
            )

        total[slot, block] *= norm_scale

    pairs_in = members // 2
    per_group = quads * pairs_in

    def landing(way, pair):
        return pltpu.make_async_remote_copy(
            src_ref=sent.at[pair],
            dst_ref=landed.at[way, pair],
            send_sem=send_sem.at[pair],
            recv_sem=recv_sem.at[way, pair],
            device_id={"win": place + 1 - 2 * way},
            device_id_type=pl.DeviceIdType.MESH,
        )

    def add_landed(way, pair, slot, base):
        landing(way, pair).wait_recv()
        coded = landed[way, pair].astype(jnp.int32)
        for member in range(2):
            part_rows = slice(base + member * ROWS, base + (member + 1) * ROWS)
            total[slot, part_rows] += decode(coded[member * ROWS : (member + 1) * ROWS])

    def pair_at(way, turn):
        group = jnp.where(way == 0, last - turn // per_group, turn // per_group)
        return group * per_group + lax.rem(turn, per_group)

    between = (place > 0) & (place < last)
    first_way = jnp.where(2 * place < windows, 0, 1)

    @pl.when(between)
    def _():
        @pl.loop(0, quads)
        def _(inner):
            correlate(place * quads + inner, inner)

    @pl.loop(0, 2 * last * quads)
    def _(slot):
        stage = slot // (2 * quads)
        inner = lax.rem(slot // 2, quads)
        way = lax.rem(slot + first_way, 2)
        group = jnp.where(way == 0, last - stage, stage)

        @pl.when(jnp.where(way == 0, group > place, group < place))
        def _():
            quad = group * quads + inner
            opening = (stage == 0) & (inner == 0)

            @pl.when(jnp.logical_not(opening))
            def _():
                correlate(quad, quads)

            for half in range(pairs_in):

                @pl.when(opening)
                def _():
                    correlate(quad, quads, 2 * half, 2)

                pair = quad * pairs_in + half
                turn = (stage * quads + inner) * pairs_in + half
                base = half * 2 * ROWS

                @pl.when(jnp.where(way == 0, place > 0, place < last))
                def _():
                    add_landed(way, pair, quads, base)

                coded = [code(total[quads, base + member * ROWS : base + (member + 1) * ROWS]) for member in range(2)]
                sent[pair] = jnp.concatenate(coded, axis=0).astype(jnp.int16)

                @pl.when(turn >= AHEAD)
                def _():
                    landing(way, pair_at(way, turn - AHEAD)).wait_send()

                landing(way, pair).start()

    @pl.when(jnp.logical_not(between))
    def _():
        @pl.loop(0, quads)
        def _(inner):
            correlate(place * quads + inner, inner)

    @pl.loop(0, quads)
    def _(inner):
        for half in range(pairs_in):
            pair = (place * quads + inner) * pairs_in + half
            base = half * 2 * ROWS

            @pl.when(place > 0)
            def _():
                add_landed(0, pair, inner, base)

            @pl.when(place < last)
            def _():
                add_landed(1, pair, inner, base)

        for member in range(members):
            out_ref[members * inner + member] = total[inner, member * ROWS : member * ROWS + LAGS]

    for hop in range(1, parts):
        meet(hop).wait_send()
        find(hop).wait_send()

    for way in range(2):
        turns = (place if way else last - place) * per_group

        @pl.loop(0, last * per_group)
        def _(turn):
            @pl.when((turn < turns) & (turn >= turns - AHEAD))
            def _():
                landing(way, pair_at(way, turn)).wait_send()


def shards(traces, sources, offsets):
    ch_dev, win_dev, span_len = traces.shape
    source_count = sources.size
    windows = lax.axis_size("win")
    parts = lax.axis_size("rcv")
    norm_scale = 1.0 / math.sqrt(SAMPLES * windows * win_dev)
    members = 4
    slabs = FOLD * parts // source_count
    width = span_len // slabs
    pairs = source_count // 2
    group = source_count // windows
    return pl.pallas_call(
        functools.partial(kernel, parts, windows, norm_scale, members, 2048),
        out_shape=jax.ShapeDtypeStruct((group, LAGS, ch_dev), jnp.float32),
        in_specs=[
            pl.BlockSpec(memory_space=pltpu.SMEM),
            pl.BlockSpec(memory_space=pltpu.SMEM),
            pl.BlockSpec(memory_space=pl.ANY),
        ],
        out_specs=pl.BlockSpec(memory_space=pltpu.VMEM),
        scratch_shapes=[
            pltpu.VMEM((ch_dev, span_len), traces.dtype),
            pltpu.VMEM((parts, FOLD, width), traces.dtype),
            pltpu.VMEM((parts - 1, FOLD, width), traces.dtype),
            pltpu.VMEM((parts, FOLD, width), traces.dtype),
            pltpu.VMEM((source_count, span_len), jnp.float32),
            pltpu.VMEM((source_count, span_len + LEAD), jnp.float32),
            pltpu.VMEM((group // members + 1, members * ROWS, ch_dev), jnp.float32),
            pltpu.VMEM((pairs, 2 * ROWS, ch_dev), jnp.int16),
            pltpu.VMEM((2, pairs, 2 * ROWS, ch_dev), jnp.int16),
            pltpu.SemaphoreType.DMA((slabs,)),
            pltpu.SemaphoreType.DMA((parts - 1,)),
            pltpu.SemaphoreType.DMA((parts - 1,)),
            pltpu.SemaphoreType.DMA((parts - 1,)),
            pltpu.SemaphoreType.DMA((parts - 1,)),
            pltpu.SemaphoreType.DMA((pairs,)),
            pltpu.SemaphoreType.DMA((2, pairs)),
        ],
        compiler_params=pltpu.CompilerParams(
            collective_id=0, has_side_effects=True, vmem_limit_bytes=56 * 1024 * 1024
        ),
        cost_estimate=pl.CostEstimate(
            flops=2 * source_count * ROWS * ch_dev * span_len,
            bytes_accessed=2 * ch_dev * span_len,
            transcendentals=0,
        ),
    )(sources.T, offsets, traces.reshape(ch_dev, span_len))


def solution(mesh):
    in_specs = (P("rcv", "win", None), P(), P("win"))
    out_specs = P("win", None, "rcv")
    return jax.shard_map(shards, mesh=mesh, in_specs=in_specs, out_specs=out_specs, check_vma=False)
```
